256 devices in a mesh: row: 16 (over z, y_hi), col: 16 (over y_lo, x, core).
Axes of the slice: x: 4, y: 4 (y_hi: 2, y_lo: 2; y = y_hi * 2 + y_lo), z: 8, core: 2. Of those that a mesh axis runs over, the one named last changes fastest.
Arguments:
- amplitudes: bfloat16 [8192, 49152], P('row', 'col'), may hold values from -6 to 6
- amp_mask: int32 [64, 384], P('row', 'col'), may hold values 0 or 1
- integrals: bfloat16 [49152, 2048], P(('col', 'row')), may hold values from -0.109375 to 0.109375
- int_mask: int32 [384, 16], replicated, may hold values 0 or 1
- others: float32 [2048, 8192], P('col', 'row'), may hold values from -6 to 6
- occ_energy: float32 [8192], P('row'), may hold values from -3 to -0.5
- virt_energy: float32 [2048], P('col'), may hold values from 0.5 to 3
Outputs:
- update: float32 [2048, 8192], P('col', 'row')
The draws below stay inside these ranges and needn't reach their ends.
All inputs are finite; a program needn't handle non-finite values. No bound on the sum of `amp_mask` on one device may be relied on, other than what follows from the above.
Results may differ from the reference program's by a relative error of at most 0.0003.
Values may be sent and summed in bfloat16 or wider, within the bound.
No kernel may reach another device: no remote copies, remote signals or barrier semaphores. Data moves between devices by JAX's collectives and lax.ppermute only.
A program may use at most 64 MiB of HBM per device.

```python
import jax
import jax.numpy as jnp
from jax import lax

TILE = 128
OT_DEV = 4
KT_DEV = 24
OTILES = 64
KTILES = 384
BTILES = 16
ROWS = 8192
VPAIRS = 49152
WINDOW = 2048
N_ROW = 16
N_COL = 16


def set_ends(entries, stream_key, least, largest):
    longest = entries.shape.index(max(entries.shape))
    spots = []
    for shift in (0, 1):
        where = [jax.random.randint(jax.random.fold_in(stream_key, axis), (), 0, length) for axis, length in enumerate(entries.shape)]
        where[longest] = (where[longest] + shift) % entries.shape[longest]
        spots.append(tuple(where))
    return entries.at[spots[0]].set(least).at[spots[1]].set(largest)


def with_spikes(result, key, source, target, blocks, factor):
    owner, partner = [(jnp.arange(result.shape[position]) // (result.shape[position] // blocks)).reshape([-1 if axis == position else 1 for axis in range(result.ndim)]) for position in (source, target)]
    chosen = jax.random.permutation(key, blocks)[partner]
    strong = (owner == chosen) | (owner == (partner + blocks // 2) % blocks)
    return jnp.where(strong, factor * result, result)


def block_levels(rng, shape, split, smallest, high):
    level = 1.0
    for position, blocks in split:
        draws = jax.random.uniform(jax.random.fold_in(jax.random.fold_in(rng, 6), position), (blocks,), jnp.float32, smallest / len(split), high / len(split))
        level = level * jnp.repeat(jnp.exp(draws), shape[position] // blocks).reshape((-1,) + (1,) * (len(shape) - 1 - position))
    return level


def normal_values(rng, shape, deviation, bound, split=(), kind=jnp.bfloat16):
    result = jax.random.normal(rng, shape, jnp.float32) * deviation
    if len(split) > 0:
        result = block_levels(rng, shape, split, -0.22, 0.18) * result
    return jnp.clip(result, min=-bound, max=bound).astype(kind)


def gaussian_with(stream_key, shape, spread, most, split, heavy, held_as=jnp.bfloat16):
    array = spread * jax.random.normal(stream_key, shape, jnp.float32)
    if split:
        array = array * block_levels(stream_key, shape, split, -0.22, 0.18)
    return jnp.clip(with_spikes(array, jax.random.fold_in(stream_key, 3), *heavy), -most, most).astype(held_as)


def setup_inputs(seed: int = 0) -> dict:
    seeds = jax.random.split(jax.random.key(seed), 8)
    amplitudes = normal_values(seeds[0], (ROWS, VPAIRS), 1.0, 6.0, ((0, 16), (1, 16)))
    amp_mask = set_ends((jax.random.randint(seeds[1], (OTILES, KTILES), 0, 4) < 3).astype(jnp.int32), jax.random.fold_in(seeds[1], 1), 0, 1)
    integrals = gaussian_with(seeds[2], (VPAIRS, WINDOW), VPAIRS ** -0.5, 0.109375, ((0, 256),), (0, 1, 256, 6.0))
    int_mask = set_ends((jax.random.randint(seeds[3], (KTILES, BTILES), 0, 4) < 3).astype(jnp.int32), jax.random.fold_in(seeds[3], 1), 0, 1)
    others = normal_values(seeds[4], (WINDOW, ROWS), 1.0, 6.0, ((0, 16), (1, 16)), jnp.float32)
    occ_energy = jnp.clip(-3.0 + 2.5 * jax.random.uniform(seeds[5], (ROWS,), jnp.float32) ** block_levels(seeds[5], (ROWS,), ((0, 16),), -0.2, 0.2), -3.0, -0.5)
    virt_energy = jnp.clip(0.5 + 2.5 * jax.random.uniform(seeds[6], (WINDOW,), jnp.float32) ** block_levels(seeds[6], (WINDOW,), ((0, 16),), -0.2, 0.2), 0.5, 3.0)
    return {"amplitudes": amplitudes, "amp_mask": amp_mask, "integrals": integrals, "int_mask": int_mask, "others": others, "occ_energy": occ_energy, "virt_energy": virt_energy}


def expand(mask):
    ones = mask.astype(jnp.bfloat16)
    return jnp.repeat(jnp.repeat(ones, TILE, axis=0), TILE, axis=1)


def reference(amplitudes, amp_mask, integrals, int_mask, others, occ_energy, virt_energy):
    masked_int = integrals * expand(int_mask)
    blocks = amplitudes.reshape(N_ROW, OT_DEV * TILE, KT_DEV * TILE * N_COL)
    mask_blocks = amp_mask.reshape(N_ROW, OT_DEV, KT_DEV * N_COL)
    group_width = KT_DEV * TILE

    def one_block(paired):
        amp_block, mask_block = paired
        masked_amp = amp_block * expand(mask_block)

        def add_group(total, group):
            start = (group * group_width).astype(jnp.int32)
            left = lax.dynamic_slice_in_dim(masked_amp, start, group_width, 1)
            right = lax.dynamic_slice_in_dim(masked_int, start, group_width, 0)
            partial_value = jnp.dot(left, right, preferred_element_type=jnp.float32)
            return total + partial_value, None

        initial = jnp.zeros((OT_DEV * TILE, WINDOW), jnp.float32)
        total, unused = lax.scan(add_group, initial, jnp.arange(N_COL, dtype=jnp.int32))
        return total

    ladder = lax.map(one_block, (blocks, mask_blocks)).reshape(ROWS, WINDOW).T
    denominators = virt_energy[:, None] - occ_energy[None, :]
    return (others + ladder) / denominators
```

```python
import functools

import jax
import jax.numpy as jnp
from jax import lax
from jax.experimental import pallas as pl
from jax.experimental.pallas import tpu as pltpu
from jax.sharding import Mesh, PartitionSpec as P

TILE = 128
HALF = 64
NZ, NX = 8, 4
OFFSETS = (0, -1, 1, -2, 2, -3, 3, 4)
CHAINS = (
    ((2, 0), (2, 1)),
    ((1, 1), (3, 1)),
    ((1, 0), (3, 0)),
    ((0, 1), (0, 0)),
)
BF16, F32 = jnp.bfloat16, jnp.float32
VMEM_LIMIT = 56 * 1024 * 1024


def whole(space=pltpu.VMEM):
    return pl.BlockSpec(memory_space=space)


def params():
    return pltpu.CompilerParams(vmem_limit_bytes=VMEM_LIMIT)


def column_of():
    return (lax.axis_index("yl") * NX + lax.axis_index("x")) * 2 + lax.axis_index("c")


def keep_where(flag, value):
    return jnp.where(flag != 0, value, jnp.zeros_like(value))


def integral_kernel(mask_ref, in_ref, own_ref, send_ref):
    z, yh, yl = lax.axis_index("z"), lax.axis_index("yh"), lax.axis_index("yl")
    x, c = lax.axis_index("x"), lax.axis_index("c")
    first_tile = 24 * column_of() + 3 * z
    full_rows = pl.ds(pl.multiple_of(yh * HALF, HALF), TILE)
    half_rows = pl.ds(pl.multiple_of((1 - yh) * TILE, HALF), HALF)
    for flip, out_ref in ((1, send_ref), (0, own_ref)):
        core = lax.rem(c + flip, 2)
        for chain, slots in enumerate(CHAINS):
            for slot, (dx, other) in enumerate(slots):
                tile = (lax.rem(yl + other, 2) * NX + lax.rem(x + dx, NX)) * 2 + core
                source = pl.ds(pl.multiple_of(tile * TILE, TILE), TILE)
                target = pl.ds(slot * TILE, TILE)
                out_ref[chain, :TILE, target] = keep_where(
                    mask_ref[first_tile + 2 * yh, tile], in_ref[full_rows, source]
                )
                out_ref[chain, TILE:, target] = keep_where(
                    mask_ref[first_tile + 1, tile], in_ref[half_rows, source]
                )


def prepare_integrals(integrals, int_mask):
    rows, window = integrals.shape
    out = jax.ShapeDtypeStruct((4, rows, window // 8), BF16)
    return pl.pallas_call(
        integral_kernel,
        out_shape=(out, out),
        in_specs=[whole(pltpu.SMEM), whole()],
        out_specs=(whole(), whole()),
        compiler_params=params(),
        cost_estimate=pl.CostEstimate(flops=0, bytes_accessed=2 * rows * window * 2, transcendentals=0),
        name="prepare_integrals",
    )(int_mask, integrals)


def amplitude_kernel(mask_ref, in_ref, keep_ref, send_ref):
    z, yh = lax.axis_index("z"), lax.axis_index("yh")
    low = lax.broadcasted_iota(jnp.int32, (TILE, TILE), 1) < HALF
    for block in range(in_ref.shape[0] // TILE):
        rows = pl.ds(block * TILE, TILE)

        def tile(index):
            columns = pl.ds(pl.multiple_of(index * TILE, TILE), TILE)
            return keep_where(mask_ref[block, index], in_ref[rows, columns])

        for place, offset in enumerate(OFFSETS):
            zz = lax.rem(z + (offset + NZ), NZ)
            target = pl.ds(place * TILE, TILE)
            keep_ref[rows, target] = tile(3 * zz + 2 * yh)
            send_ref[rows, target] = tile(3 * zz + 2 * (1 - yh))
        for pair in range(NZ // 2):
            first, second = (
                tile(3 * lax.rem(z + (offset + NZ), NZ) + 1).astype(F32)
                for offset in OFFSETS[2 * pair : 2 * pair + 2]
            )
            left = jnp.where(low, first, pltpu.roll(second, HALF, 1)).astype(BF16)
            right = jnp.where(low, pltpu.roll(first, HALF, 1), second).astype(BF16)
            target = pl.ds((NZ + pair) * TILE, TILE)
            keep_ref[rows, target] = jnp.where(yh == 0, left, right)
            send_ref[rows, target] = jnp.where(yh == 0, right, left)


def prepare_amplitudes(amplitudes, amp_mask):
    rows, columns = amplitudes.shape
    out = jax.ShapeDtypeStruct((rows, columns // 2), BF16)
    return pl.pallas_call(
        amplitude_kernel,
        out_shape=(out, out),
        in_specs=[whole(pltpu.SMEM), whole()],
        out_specs=(whole(), whole()),
        compiler_params=params(),
        cost_estimate=pl.CostEstimate(flops=0, bytes_accessed=4 * rows * columns, transcendentals=0),
        name="prepare_amplitudes",
    )(amp_mask, amplitudes)


def product_kernel(n_add, *refs):
    amp = refs[:2]
    pieces = refs[2:11]
    added = refs[11 : 11 + n_add]
    outs = refs[11 + n_add : 13 + n_add]
    held = refs[13 + n_add]
    rows = held.shape[1] // NZ
    for place in range(NZ):
        for group in range(2):
            if place < NZ - 1:
                piece, start = pieces[place], group * rows
            else:
                piece, start = pieces[place + group], 0
            held[group, pl.ds(place * TILE, TILE), :] = piece[pl.ds(start, TILE), :]
            held[group, pl.ds(NZ * TILE + place * HALF, HALF), :] = piece[pl.ds(start + TILE, HALF), :]
    total = jnp.dot(amp[0][...], held[0], preferred_element_type=F32)
    total += jnp.dot(amp[1][...], held[1], preferred_element_type=F32)
    first, second = total[:, :TILE], total[:, TILE:]
    if n_add:
        second = second + added[0][...] if n_add == 1 else second
    outs[0][...] = first
    outs[1][...] = second


def product(amp, pieces, added=(), name="product"):
    rows, depth = amp[0].shape
    width = pieces[0].shape[1]
    out = jax.ShapeDtypeStruct((rows, TILE), F32)
    operands = (*amp, *pieces, *added)
    return pl.pallas_call(
        functools.partial(product_kernel, len(added)),
        out_shape=(out, out),
        in_specs=[whole()] * len(operands),
        out_specs=(whole(), whole()),
        scratch_shapes=[pltpu.VMEM((2, depth, width), BF16)],
        compiler_params=params(),
        cost_estimate=pl.CostEstimate(
            flops=4 * rows * depth * width, bytes_accessed=4 * rows * depth, transcendentals=0
        ),
        name=name,
    )(*operands)


def final_kernel(total_refs, others_ref, occ_ref, virt_ref, out_ref):
    total = total_refs[0][...]
    for ref in total_refs[1:]:
        total = total + ref[...]
    ladder = total.T
    out_ref[...] = (others_ref[...] + ladder) / (virt_ref[...] - occ_ref[...])


def finish(totals, others, occ_energy, virt_energy):
    n = len(totals)

    def kernel(*refs):
        final_kernel(refs[:n], *refs[n:])

    return pl.pallas_call(
        kernel,
        out_shape=jax.ShapeDtypeStruct(others.shape, F32),
        in_specs=[whole()] * (n + 3),
        out_specs=whole(),
        compiler_params=params(),
        name="finish",
    )(*totals, others, occ_energy[None, :], virt_energy[:, None])


def shift(value, axis, size, step):
    return lax.ppermute(value, axis, [(i, (i + step) % size) for i in range(size)])


def swap_y(value, bits):
    return lax.ppermute(value, ("yh", "yl"), [(i, i ^ bits) for i in range(4)])


def ring(piece):
    up = down = piece
    pieces = [piece]
    for _ in range(3):
        up, down = shift(up, "z", NZ, 1), shift(down, "z", NZ, -1)
        pieces += [up, down]
    half = piece.shape[0] // 2
    return pieces + [shift(up[:half], "z", NZ, 1), shift(down[half:], "z", NZ, -1)]


def after(value, *others):
    return lax.optimization_barrier((value, *others))[0]


def body(amplitudes, amp_mask, integrals, int_mask, others, occ_energy, virt_energy):
    own, send = prepare_integrals(integrals, int_mask)
    received = shift(send, "c", 2, 1)

    def start_of(chain):
        return jnp.concatenate([own[chain], received[chain]], axis=0)

    gathered = [ring(start_of(0)), ring(start_of(1))]
    gathered.append(ring(after(start_of(2), gathered[0][6])))
    gathered.append(ring(after(start_of(3), gathered[1][6])))

    keep, away = prepare_amplitudes(amplitudes, amp_mask)
    here = (keep, shift(keep, "c", 2, 1))
    other_rows = swap_y(away, 2)
    there = (other_rows, shift(other_rows, "c", 2, 1))

    def along_x(value, step):
        return shift(value, "x", NX, step)

    via_up, via_down = [], []
    for amp in (here, there):
        low, high = product(amp, gathered[0])
        via_up.append(along_x(low, 1))
        via_down.append(along_x(high, -1))
    arrived = {}
    for chain in (1, 2):
        for side, amp in enumerate((here, there)):
            low, high = product(amp, gathered[chain])
            if chain == 1:
                high = high + via_down[side]
            else:
                low = low + via_up[side]
            arrived[chain, side] = (along_x(low, 1), along_x(high, -1))
    own_sums = [product(amp, gathered[3]) for amp in (here, there)]

    def summed(slot, chain, side):
        first, second = arrived[chain, side]
        return own_sums[side][slot] + first + second

    totals = [
        summed(1, 2, 0),
        swap_y(summed(0, 1, 0), 1),
        swap_y(summed(0, 1, 1), 3),
        swap_y(summed(1, 2, 1), 2),
    ]
    return finish(totals, others, occ_energy, virt_energy)


def solution(mesh):
    fine = Mesh(mesh.devices.reshape(NZ, 2, 2, NX, 2), ("z", "yh", "yl", "x", "c"))
    row, col = ("z", "yh"), ("yl", "x", "c")
    placed = (P(row, col), P(row, col), P(col + row, None), P(), P(col, row), P(row), P(col))
    return jax.shard_map(
        body, mesh=fine, in_specs=placed, out_specs=P(col, row), check_vma=False
    )
```

```python
import functools

import jax
import jax.numpy as jnp
from jax import lax
from jax.experimental import pallas as pl
from jax.experimental.pallas import tpu as pltpu
from jax.sharding import Mesh, PartitionSpec as P

TILE = 128
HALF = 64
NZ, NX = 8, 4
OFFSETS = (0, -1, 1, -2, 2, -3, 3, 4)
CHAINS = (
    ((2, 0), (2, 1)),
    ((1, 1), (3, 1)),
    ((1, 0), (3, 0)),
    ((0, 1), (0, 0)),
)
BF16, F32 = jnp.bfloat16, jnp.float32
VMEM_LIMIT = 16 * 1024 * 1024


def whole(space=pltpu.VMEM):
    return pl.BlockSpec(memory_space=space)


def params():
    return pltpu.CompilerParams(vmem_limit_bytes=VMEM_LIMIT)


def column_of():
    return (lax.axis_index("yl") * NX + lax.axis_index("x")) * 2 + lax.axis_index("c")


def keep_where(flag, value):
    return jnp.where(flag != 0, value, jnp.zeros_like(value))


def integral_kernel(mask_ref, in_ref, *out_refs):
    yh, yl = lax.axis_index("yh"), lax.axis_index("yl")
    x, c = lax.axis_index("x"), lax.axis_index("c")
    full_rows = pl.ds(pl.multiple_of(yh * HALF, HALF), TILE)
    half_rows = pl.ds(pl.multiple_of((1 - yh) * TILE, HALF), HALF)
    for flip in (1, 0):
        core = lax.rem(c + flip, 2)
        for chain, slots in enumerate(CHAINS):
            out_ref = out_refs[chain // 2].at[chain % 2] if flip else out_refs[2 + chain]
            for slot, (dx, other) in enumerate(slots):
                tile = (lax.rem(yl + other, 2) * NX + lax.rem(x + dx, NX)) * 2 + core
                source = pl.ds(pl.multiple_of(tile * TILE, TILE), TILE)
                target = pl.ds(slot * TILE, TILE)
                out_ref[:TILE, target] = keep_where(mask_ref[2 * yh, tile], in_ref[full_rows, source])
                out_ref[TILE:, target] = keep_where(mask_ref[1, tile], in_ref[half_rows, source])


def prepare_integrals(integrals, int_mask):
    rows, window = integrals.shape
    first_tile = 24 * column_of() + 3 * lax.axis_index("z")
    mask_rows = lax.dynamic_slice_in_dim(int_mask, first_tile, 3, axis=0)
    piece = jax.ShapeDtypeStruct((rows, window // 8), BF16)
    pair = jax.ShapeDtypeStruct((2, rows, window // 8), BF16)
    outs = pl.pallas_call(
        integral_kernel,
        out_shape=(pair,) * 2 + (piece,) * 4,
        in_specs=[whole(pltpu.SMEM), whole()],
        out_specs=(whole(),) * 6,
        compiler_params=params(),
        cost_estimate=pl.CostEstimate(flops=0, bytes_accessed=2 * rows * window * 2, transcendentals=0),
        name="prepare_integrals",
    )(mask_rows, integrals)
    return outs[:2], outs[2:]


def amplitude_kernel(mask_ref, in_ref, keep_ref, send_ref):
    z, yh, block = lax.axis_index("z"), lax.axis_index("yh"), pl.program_id(0)
    low = lax.broadcasted_iota(jnp.int32, (TILE, TILE), 1) < HALF

    def tile(index):
        columns = pl.ds(pl.multiple_of(index * TILE, TILE), TILE)
        return keep_where(mask_ref[block, index], in_ref[:, columns])

    for place, offset in enumerate(OFFSETS):
        zz = lax.rem(z + (offset + NZ), NZ)
        target = pl.ds(place * TILE, TILE)
        keep_ref[:, target] = tile(3 * zz + 2 * yh)
        send_ref[:, target] = tile(3 * zz + 2 * (1 - yh))
    for pair in range(NZ // 2):
        first, second = (
            tile(3 * lax.rem(z + (offset + NZ), NZ) + 1).astype(F32)
            for offset in OFFSETS[2 * pair : 2 * pair + 2]
        )
        left = jnp.where(low, first, pltpu.roll(second, HALF, 1)).astype(BF16)
        right = jnp.where(low, pltpu.roll(first, HALF, 1), second).astype(BF16)
        target = pl.ds((NZ + pair) * TILE, TILE)
        keep_ref[:, target] = jnp.where(yh == 0, left, right)
        send_ref[:, target] = jnp.where(yh == 0, right, left)


def prepare_amplitudes(amplitudes, amp_mask):
    rows, columns = amplitudes.shape
    out = jax.ShapeDtypeStruct((rows, columns // 2), BF16)
    return pl.pallas_call(
        amplitude_kernel,
        grid=(rows // TILE,),
        out_shape=(out, out),
        in_specs=[whole(pltpu.SMEM), pl.BlockSpec((TILE, columns), lambda i: (i, 0))],
        out_specs=(pl.BlockSpec((TILE, columns // 2), lambda i: (i, 0)),) * 2,
        compiler_params=params(),
        cost_estimate=pl.CostEstimate(flops=0, bytes_accessed=4 * rows * columns, transcendentals=0),
        name="prepare_amplitudes",
    )(amp_mask, amplitudes)


def product_kernel(sides, places, *refs):
    amps, refs = refs[: 2 * sides], refs[2 * sides :]
    pieces, refs = refs[:NZ], refs[NZ:]
    added, outs, held = refs[: len(places)], refs[len(places) : -1], refs[-1]
    rows = pieces[0].shape[0] // 2
    for place in range(NZ):
        for group in range(2):
            start = group * rows
            held[group, pl.ds(place * TILE, TILE), :] = pieces[place][pl.ds(start, TILE), :]
            held[group, pl.ds(NZ * TILE + place * HALF, HALF), :] = pieces[place][pl.ds(start + TILE, HALF), :]
    for side in range(sides):
        total = jnp.dot(amps[2 * side][...], held[0], preferred_element_type=F32)
        total += jnp.dot(amps[2 * side + 1][...], held[1], preferred_element_type=F32)
        for slot in range(2):
            part = total[:, slot * TILE : (slot + 1) * TILE]
            for ref, place in zip(added, places):
                if place == (side, slot):
                    part = part + ref[...]
            outs[2 * side + slot][...] = part


def product(amps, pieces, added=(), name="product"):
    rows, depth = amps[0][0].shape
    width = pieces[0].shape[1]
    sides = len(amps)
    out = jax.ShapeDtypeStruct((rows, TILE), F32)
    operands = [a for amp in amps for a in amp] + list(pieces) + [value for _, value in added]
    outs = pl.pallas_call(
        functools.partial(product_kernel, sides, tuple(place for place, _ in added)),
        out_shape=(out,) * (2 * sides),
        in_specs=[whole()] * len(operands),
        out_specs=(whole(),) * (2 * sides),
        scratch_shapes=[pltpu.VMEM((2, depth, width), BF16)],
        compiler_params=params(),
        cost_estimate=pl.CostEstimate(
            flops=4 * sides * rows * depth * width, bytes_accessed=4 * rows * depth, transcendentals=0
        ),
        name=name,
    )(*operands)
    return [outs[2 * side : 2 * side + 2] for side in range(sides)]


def finish_kernel(*refs):
    totals, (others_ref, occ_ref, virt_ref, out_ref) = refs[:-4], refs[-4:]
    total = totals[0][...]
    for ref in totals[1:]:
        total = total + ref[...]
    virt = jnp.broadcast_to(virt_ref[...], (TILE, TILE)).T
    for block in range(out_ref.shape[1] // TILE):
        columns = pl.ds(block * TILE, TILE)
        ladder = total[block * TILE : (block + 1) * TILE, :].T
        out_ref[:, columns] = (others_ref[:, columns] + ladder) / (virt - occ_ref[:, columns])


def finish(totals, others, occ_energy, virt_energy):
    return pl.pallas_call(
        finish_kernel,
        out_shape=jax.ShapeDtypeStruct(others.shape, F32),
        in_specs=[whole()] * (len(totals) + 3),
        out_specs=whole(),
        compiler_params=params(),
        name="finish",
    )(*totals, others, occ_energy[None, :], virt_energy[None, :])


def shift(value, axis, size, step):
    return lax.ppermute(value, axis, [(i, (i + step) % size) for i in range(size)])


def swap_y(value, bits):
    return lax.ppermute(value, ("yh", "yl"), [(i, i ^ bits) for i in range(4)])


def along_x(value, step):
    return shift(value, "x", NX, step)


def tie(*values):
    return lax.optimization_barrier(values)


def body(amplitudes, amp_mask, integrals, int_mask, others, occ_energy, virt_energy):
    send, own = prepare_integrals(integrals, int_mask)
    received = [shift(value, "c", 2, 1) for value in send]
    starts = [
        jnp.concatenate([own[chain], received[chain // 2][chain % 2]], axis=0) for chain in range(4)
    ]

    def step(up, down):
        return shift(up, "z", NZ, 1), shift(down, "z", NZ, -1)

    first = [starts[0]], [starts[1]]
    ends = [(starts[0],) * 2, (starts[1],) * 2]
    amplitudes, starts[0] = tie(amplitudes, starts[0])
    for _ in range(3):
        for chain in range(2):
            ends[chain] = step(*ends[chain])
            first[chain].extend(ends[chain])
    keep, away = prepare_amplitudes(amplitudes, amp_mask)
    here = (keep, shift(keep, "c", 2, 1))
    other_rows = swap_y(away, 2)

    second, third = tie(starts[2], *ends[0]), tie(starts[3], *ends[1])
    first[0].append(shift(second[1], "z", NZ, 1))
    first[1].append(shift(third[2], "z", NZ, -1))
    last = [second[0]], [third[0]]
    ends = [step(second[0], second[0]), step(third[0], third[0])]
    for chain in range(2):
        last[chain].extend(ends[chain])

    ((low, high),) = product([here], first[0], name="product_a0")
    low, high, *ends[0] = tie(low, high, *ends[0])
    up_here, down_here = along_x(low, 1), along_x(high, -1)
    ends[0] = step(*ends[0])
    last[0].extend(ends[0])
    ends[1] = step(*ends[1])
    last[1].extend(ends[1])

    ((low, high),) = product([here], first[1], [((0, 1), down_here)], name="product_b0")
    low, high, other_rows, *ends[0] = tie(low, high, other_rows, *ends[0])
    near_here = along_x(low, 1), along_x(high, -1)
    there = (other_rows, shift(other_rows, "c", 2, 1))
    ends[0] = step(*ends[0])
    last[0].extend(ends[0])
    ends[1] = step(*ends[1])
    last[1].extend(ends[1])

    ((low, high),) = product([there], first[0], name="product_a1")
    low, high, *ends[0] = tie(low, high, *ends[0])
    up_there, down_there = along_x(low, 1), along_x(high, -1)
    last[0].append(shift(ends[0][0], "z", NZ, 1))
    last[1].append(shift(ends[1][1], "z", NZ, -1))
    ((low, high),) = product([there], first[1], [((0, 1), down_there)], name="product_b1")
    near_there = along_x(low, 1), along_x(high, -1)

    third = product(
        [there, here], last[0], [((0, 0), up_there), ((1, 0), up_here)], name="product_c"
    )
    (there_up, there_down), (here_up, here_down) = [
        (along_x(low, 1), along_x(high, -1)) for low, high in third
    ]
    added = [((0, 0), value) for value in near_there] + [((1, 0), value) for value in near_here]
    (far_there, own_there), (far_here, own_here) = product(
        [there, here], last[1], added, name="product_d"
    )
    totals = [
        own_here,
        here_up,
        here_down,
        swap_y(far_here, 1),
        swap_y(far_there, 3),
        swap_y(own_there + there_up + there_down, 2),
    ]
    return finish(totals, others, occ_energy, virt_energy)


def solution(mesh):
    fine = Mesh(mesh.devices.reshape(NZ, 2, 2, NX, 2), ("z", "yh", "yl", "x", "c"))
    row, col = ("z", "yh"), ("yl", "x", "c")
    placed = (P(row, col), P(row, col), P(col + row, None), P(), P(col, row), P(row), P(col))
    return jax.shard_map(
        body, mesh=fine, in_specs=placed, out_specs=P(col, row), check_vma=False
    )
```

```python
import functools

import jax
import jax.numpy as jnp
from jax import lax
from jax.experimental import pallas as pl
from jax.experimental.pallas import tpu as pltpu
from jax.sharding import Mesh, PartitionSpec as P

TILE = 128
HALF = 64
NZ, NX = 8, 4
OFFSETS = (0, -1, 1, -2, 2, -3, 3, 4)
CHAINS = (
    ((1, 0), (3, 0), (2, 0), (2, 1)),
    ((1, 1), (3, 1), (0, 1), (0, 0)),
)
BF16, F32 = jnp.bfloat16, jnp.float32
VMEM_LIMIT = 16 * 1024 * 1024


def whole(space=pltpu.VMEM):
    return pl.BlockSpec(memory_space=space)


def params():
    return pltpu.CompilerParams(vmem_limit_bytes=VMEM_LIMIT)


def column_of():
    return (lax.axis_index("yl") * NX + lax.axis_index("x")) * 2 + lax.axis_index("c")


def keep_where(flag, value):
    return jnp.where(flag != 0, value, jnp.zeros_like(value))


def integral_kernel(mask_ref, in_ref, send_ref, *own_refs):
    yh, yl = lax.axis_index("yh"), lax.axis_index("yl")
    x, c = lax.axis_index("x"), lax.axis_index("c")
    full_rows = pl.ds(pl.multiple_of(yh * HALF, HALF), TILE)
    half_rows = pl.ds(pl.multiple_of((1 - yh) * TILE, HALF), HALF)
    for flip in (1, 0):
        core = lax.rem(c + flip, 2)
        sent = 0
        for chain, slots in enumerate(CHAINS):
            for slot, (dx, other) in enumerate(slots):
                tile = (lax.rem(yl + other, 2) * NX + lax.rem(x + dx, NX)) * 2 + core
                source = pl.ds(pl.multiple_of(tile * TILE, TILE), TILE)
                out_ref, place = (send_ref, sent) if flip else (own_refs[chain], slot)
                target = pl.ds(place * TILE, TILE)
                out_ref[:TILE, target] = keep_where(mask_ref[2 * yh, tile], in_ref[full_rows, source])
                out_ref[TILE:, target] = keep_where(mask_ref[1, tile], in_ref[half_rows, source])
                sent += 1


def prepare_integrals(integrals, int_mask):
    rows, window = integrals.shape
    first_tile = 24 * column_of() + 3 * lax.axis_index("z")
    mask_rows = lax.dynamic_slice_in_dim(int_mask, first_tile, 3, axis=0)
    widths = (window // 2,) + tuple(TILE * len(slots) for slots in CHAINS)
    outs = pl.pallas_call(
        integral_kernel,
        out_shape=tuple(jax.ShapeDtypeStruct((rows, width), BF16) for width in widths),
        in_specs=[whole(pltpu.SMEM), whole()],
        out_specs=(whole(),) * len(widths),
        compiler_params=params(),
        cost_estimate=pl.CostEstimate(flops=0, bytes_accessed=2 * rows * window * 2, transcendentals=0),
        name="prepare_integrals",
    )(mask_rows, integrals)
    return outs[0], outs[1:]


def amplitude_kernel(flip, mask_ref, in_ref, out_ref):
    z, block = lax.axis_index("z"), pl.program_id(0)
    yh = lax.rem(lax.axis_index("yh") + flip, 2)
    low = lax.broadcasted_iota(jnp.int32, (TILE, TILE), 1) < HALF

    def tile(index):
        columns = pl.ds(pl.multiple_of(index * TILE, TILE), TILE)
        return keep_where(mask_ref[block, index], in_ref[:, columns])

    sources = [lax.rem(z + (offset + NZ), NZ) for offset in OFFSETS]
    for place, zz in enumerate(sources):
        out_ref[:, pl.ds(place * TILE, TILE)] = tile(3 * zz + 2 * yh)
    for pair in range(NZ // 2):
        first, second = (tile(3 * zz + 1).astype(F32) for zz in sources[2 * pair : 2 * pair + 2])
        left = jnp.where(low, first, pltpu.roll(second, HALF, 1))
        right = jnp.where(low, pltpu.roll(first, HALF, 1), second)
        out_ref[:, pl.ds((NZ + pair) * TILE, TILE)] = jnp.where(yh == 0, left, right).astype(BF16)


def prepare_amplitudes(amplitudes, amp_mask, flip):
    rows, columns = amplitudes.shape
    return pl.pallas_call(
        functools.partial(amplitude_kernel, flip),
        grid=(rows // TILE,),
        out_shape=jax.ShapeDtypeStruct((rows, columns // 2), BF16),
        in_specs=[whole(pltpu.SMEM), pl.BlockSpec((TILE, columns), lambda i: (i, 0))],
        out_specs=pl.BlockSpec((TILE, columns // 2), lambda i: (i, 0)),
        compiler_params=params(),
        cost_estimate=pl.CostEstimate(flops=0, bytes_accessed=3 * rows * columns, transcendentals=0),
        name="prepare_amplitudes",
    )(amp_mask, amplitudes)


def product_kernel(half, joined, *refs):
    amps, pieces, outs, held = refs[:2], refs[2 : 2 + NZ], refs[2 + NZ : -1], refs[-1]
    rows, width = pieces[0].shape[0] // 2, held.shape[2]
    columns = pl.ds(half * width, width)
    for place, piece in enumerate(pieces):
        for group in range(2):
            start = group * rows
            full, rest = pl.ds(place * TILE, TILE), pl.ds(NZ * TILE + place * HALF, HALF)
            held[group, full, :] = piece[pl.ds(start, TILE), columns]
            held[group, rest, :] = piece[pl.ds(start + TILE, HALF), columns]
    rows = amps[0].shape[0] // 2
    for side in range(2):
        mine = pl.ds(side * rows, rows)
        total = jnp.dot(amps[0][mine, :], held[0], preferred_element_type=F32)
        total += jnp.dot(amps[1][mine, :], held[1], preferred_element_type=F32)
        for slot in range(2):
            part = total[:, slot * TILE : (slot + 1) * TILE]
            if joined:
                outs[slot][side] = part
            else:
                outs[2 * side + slot][...] = part


def product(amps, pieces, half, joined=False, name="product"):
    rows, depth = amps[0].shape
    rows, width = rows // 2, 2 * TILE
    if joined:
        out_shape = (jax.ShapeDtypeStruct((2, rows, TILE), F32),) * 2
    else:
        out_shape = (jax.ShapeDtypeStruct((rows, TILE), F32),) * 4
    operands = list(amps) + list(pieces)
    outs = pl.pallas_call(
        functools.partial(product_kernel, half, joined),
        out_shape=out_shape,
        in_specs=[whole()] * len(operands),
        out_specs=(whole(),) * len(out_shape),
        scratch_shapes=[pltpu.VMEM((2, depth, width), BF16)],
        compiler_params=params(),
        cost_estimate=pl.CostEstimate(
            flops=8 * rows * depth * width, bytes_accessed=8 * rows * depth, transcendentals=0
        ),
        name=name,
    )(*operands)
    return outs if joined else (outs[:2], outs[2:])


def finish_kernel(*refs):
    totals, (others_ref, occ_ref, virt_ref, out_ref) = refs[:-4], refs[-4:]
    total = totals[0][...]
    for ref in totals[1:]:
        total = total + ref[...]
    virt = jnp.broadcast_to(virt_ref[...], (TILE, TILE)).T
    for block in range(out_ref.shape[1] // TILE):
        columns = pl.ds(block * TILE, TILE)
        ladder = total[block * TILE : (block + 1) * TILE, :].T
        out_ref[:, columns] = (others_ref[:, columns] + ladder) / (virt - occ_ref[:, columns])


def finish(totals, others, occ_energy, virt_energy):
    return pl.pallas_call(
        finish_kernel,
        out_shape=jax.ShapeDtypeStruct(others.shape, F32),
        in_specs=[whole()] * (len(totals) + 3),
        out_specs=whole(),
        compiler_params=params(),
        name="finish",
    )(*totals, others, occ_energy[None, :], virt_energy[None, :])


def shift(value, axis, size, step):
    return lax.ppermute(value, axis, [(i, (i + step) % size) for i in range(size)])


def swap_y(value, bits):
    return lax.ppermute(value, ("yh", "yl"), [(i, i ^ bits) for i in range(4)])


def along_x(value, step):
    return shift(value, "x", NX, step)


def after(value, *others):
    return lax.optimization_barrier((value, *others))[0]


def body(amplitudes, amp_mask, integrals, int_mask, others, occ_energy, virt_energy):
    def join(*values):
        return jnp.concatenate(values, axis=0)

    send, own = prepare_integrals(integrals, int_mask)
    received = shift(send, "c", 2, 1)
    width = own[0].shape[1]
    starts = [join(own[i], received[:, i * width : (i + 1) * width]) for i in range(2)]
    away = prepare_amplitudes(amplitudes, after(amp_mask, *starts), 1)
    keep = prepare_amplitudes(amplitudes, after(amp_mask, away), 0)
    other_rows = swap_y(away, 2)

    chains = [[start] for start in starts]
    ends = [[start, start] for start in starts]
    for step in range(3):
        ends = [[shift(up, "z", NZ, 1), shift(down, "z", NZ, -1)] for up, down in ends]
        if step == 0:
            ends = [[after(up, away, keep), after(down, away, keep)] for up, down in ends]
        for chain, pair in zip(chains, ends):
            chain.extend(pair)
    mine = after(join(other_rows, keep), *ends[0], *ends[1])
    chains[0].append(shift(ends[0][0], "z", NZ, 1))
    chains[1].append(shift(ends[1][1], "z", NZ, -1))
    amps = mine, shift(mine, "c", 2, 1)

    c_there, c_here = [
        (along_x(low, 1), along_x(high, -1))
        for low, high in product(amps, chains[0], 0, name="product_c")
    ]
    up, down = product(amps, chains[1], 0, joined=True, name="product_b")
    near = along_x(up, 1), along_x(down, -1)
    a_there, a_here = product(amps, chains[0], 1, name="product_a")
    far = a_here[0] + swap_y(a_here[1], 1) + swap_y(a_there[1], 3) + swap_y(a_there[0], 2)
    far = along_x(far, 2)
    d_there, d_here = product(amps, chains[1], 1, name="product_d")
    totals = [
        d_here[1],
        far,
        *c_here,
        swap_y(d_there[1] + c_there[0] + c_there[1], 2),
        swap_y(d_here[0] + near[0][1] + near[1][1], 1),
        swap_y(d_there[0] + near[0][0] + near[1][0], 3),
    ]
    return finish(totals, others, occ_energy, virt_energy)


def solution(mesh):
    fine = Mesh(mesh.devices.reshape(NZ, 2, 2, NX, 2), ("z", "yh", "yl", "x", "c"))
    row, col = ("z", "yh"), ("yl", "x", "c")
    placed = (P(row, col), P(row, col), P(col + row, None), P(), P(col, row), P(row), P(col))
    return jax.shard_map(
        body, mesh=fine, in_specs=placed, out_specs=P(col, row), check_vma=False
    )
```

```python
import functools

import jax
import jax.numpy as jnp
from jax import lax
from jax.experimental import pallas as pl
from jax.experimental.pallas import tpu as pltpu
from jax.sharding import Mesh, PartitionSpec as P

TILE = 128
HALF = 64
NZ, NX = 8, 4
OFFSETS = (0, -1, 1, -2, 2, -3, 3, 4)
CHAINS = (
    ((1, 0), (3, 0), (2, 0), (2, 1)),
    ((1, 1), (3, 1), (0, 1), (0, 0)),
)
BF16, F32 = jnp.bfloat16, jnp.float32
VMEM_LIMIT = 16 * 1024 * 1024


def whole(space=pltpu.VMEM):
    return pl.BlockSpec(memory_space=space)


def params():
    return pltpu.CompilerParams(vmem_limit_bytes=VMEM_LIMIT)


def column_of():
    return (lax.axis_index("yl") * NX + lax.axis_index("x")) * 2 + lax.axis_index("c")


def keep_where(flag, value):
    return jnp.where(flag != 0, value, jnp.zeros_like(value))


def integral_kernel(mask_ref, in_ref, *refs):
    (send_ref, *own_refs), kept = refs[:-1], refs[-1]
    yh, yl = lax.axis_index("yh"), lax.axis_index("yl")
    x, c = lax.axis_index("x"), lax.axis_index("c")
    full_rows = pl.ds(pl.multiple_of(yh * HALF, HALF), TILE)
    half_rows = pl.ds(pl.multiple_of((1 - yh) * TILE, HALF), HALF)
    first_tile = 24 * column_of() + 3 * lax.axis_index("z")
    index = lax.broadcasted_iota(jnp.int32, mask_ref.shape, 1)
    for which, row_tile in enumerate((first_tile + 2 * yh, first_tile + 1)):
        picked = jnp.where(index == row_tile, mask_ref[...], 0).astype(F32)
        kept[which] = jnp.broadcast_to(jnp.sum(picked, axis=1, keepdims=True), kept.shape[1:])

    def masked(rows, tile, which):
        columns = pl.ds(pl.multiple_of(tile * TILE, TILE), TILE)
        return in_ref[rows, columns] * kept[which, pl.ds(tile, 1), :].astype(BF16)

    for flip in (1, 0):
        core = lax.rem(c + flip, 2)
        sent = 0
        for chain, slots in enumerate(CHAINS):
            for slot, (dx, other) in enumerate(slots):
                tile = (lax.rem(yl + other, 2) * NX + lax.rem(x + dx, NX)) * 2 + core
                out_ref, place = (send_ref, sent) if flip else (own_refs[chain], slot)
                target = pl.ds(place * TILE, TILE)
                out_ref[:TILE, target] = masked(full_rows, tile, 0)
                out_ref[TILE:, target] = masked(half_rows, tile, 1)
                sent += 1


def prepare_integrals(integrals, int_mask):
    rows, window = integrals.shape
    widths = (window // 2,) + tuple(TILE * len(slots) for slots in CHAINS)
    outs = pl.pallas_call(
        integral_kernel,
        out_shape=tuple(jax.ShapeDtypeStruct((rows, width), BF16) for width in widths),
        in_specs=[whole(), whole()],
        out_specs=(whole(),) * len(widths),
        scratch_shapes=[pltpu.VMEM((2, int_mask.shape[1], TILE), F32)],
        compiler_params=params(),
        cost_estimate=pl.CostEstimate(flops=0, bytes_accessed=2 * rows * window * 2, transcendentals=0),
        name="prepare_integrals",
    )(int_mask.T, integrals)
    return outs[0], outs[1:]


def amplitude_kernel(flip, mask_ref, in_ref, out_ref):
    z, block = lax.axis_index("z"), pl.program_id(0)
    yh = lax.rem(lax.axis_index("yh") + flip, 2)
    low = lax.broadcasted_iota(jnp.int32, (TILE, TILE), 1) < HALF

    def tile(index):
        columns = pl.ds(pl.multiple_of(index * TILE, TILE), TILE)
        return keep_where(mask_ref[block, index], in_ref[:, columns])

    sources = [lax.rem(z + (offset + NZ), NZ) for offset in OFFSETS]
    for place, zz in enumerate(sources):
        out_ref[:, pl.ds(place * TILE, TILE)] = tile(3 * zz + 2 * yh)
    for pair in range(NZ // 2):
        first, second = (tile(3 * zz + 1).astype(F32) for zz in sources[2 * pair : 2 * pair + 2])
        left = jnp.where(low, first, pltpu.roll(second, HALF, 1))
        right = jnp.where(low, pltpu.roll(first, HALF, 1), second)
        out_ref[:, pl.ds((NZ + pair) * TILE, TILE)] = jnp.where(yh == 0, left, right).astype(BF16)


def prepare_amplitudes(amplitudes, amp_mask, flip):
    rows, columns = amplitudes.shape
    return pl.pallas_call(
        functools.partial(amplitude_kernel, flip),
        grid=(rows // TILE,),
        out_shape=jax.ShapeDtypeStruct((rows, columns // 2), BF16),
        in_specs=[whole(pltpu.SMEM), pl.BlockSpec((TILE, columns), lambda i: (i, 0))],
        out_specs=pl.BlockSpec((TILE, columns // 2), lambda i: (i, 0)),
        compiler_params=params(),
        cost_estimate=pl.CostEstimate(flops=0, bytes_accessed=3 * rows * columns, transcendentals=0),
        name="prepare_amplitudes",
    )(amp_mask, amplitudes)


def product_kernel(half, joined, *refs):
    amps, pieces, outs, held = refs[:2], refs[2 : 2 + NZ], refs[2 + NZ : -1], refs[-1]
    rows, width = pieces[0].shape[0] // 2, held.shape[2]
    columns = pl.ds(half * width, width)
    for place, piece in enumerate(pieces):
        for group in range(2):
            start = group * rows
            full, rest = pl.ds(place * TILE, TILE), pl.ds(NZ * TILE + place * HALF, HALF)
            held[group, full, :] = piece[pl.ds(start, TILE), columns]
            held[group, rest, :] = piece[pl.ds(start + TILE, HALF), columns]
    rows = amps[0].shape[0] // 2
    for side in range(2):
        mine = pl.ds(side * rows, rows)
        total = jnp.dot(amps[0][mine, :], held[0], preferred_element_type=F32)
        total += jnp.dot(amps[1][mine, :], held[1], preferred_element_type=F32)
        for slot in range(2):
            part = total[:, slot * TILE : (slot + 1) * TILE]
            if joined:
                outs[slot][side] = part
            else:
                outs[2 * side + slot][...] = part


def product(amps, pieces, half, joined=False, name="product"):
    rows, depth = amps[0].shape
    rows, width = rows // 2, 2 * TILE
    if joined:
        out_shape = (jax.ShapeDtypeStruct((2, rows, TILE), F32),) * 2
    else:
        out_shape = (jax.ShapeDtypeStruct((rows, TILE), F32),) * 4
    operands = list(amps) + list(pieces)
    outs = pl.pallas_call(
        functools.partial(product_kernel, half, joined),
        out_shape=out_shape,
        in_specs=[whole()] * len(operands),
        out_specs=(whole(),) * len(out_shape),
        scratch_shapes=[pltpu.VMEM((2, depth, width), BF16)],
        compiler_params=params(),
        cost_estimate=pl.CostEstimate(
            flops=8 * rows * depth * width, bytes_accessed=8 * rows * depth, transcendentals=0
        ),
        name=name,
    )(*operands)
    return outs if joined else (outs[:2], outs[2:])


def finish_kernel(*refs):
    totals, (others_ref, occ_ref, virt_ref, out_ref) = refs[:-4], refs[-4:]
    total = totals[0][...]
    for ref in totals[1:]:
        total = total + ref[...]
    virt = jnp.broadcast_to(virt_ref[...], (TILE, TILE)).T
    for block in range(out_ref.shape[1] // TILE):
        columns = pl.ds(block * TILE, TILE)
        ladder = total[block * TILE : (block + 1) * TILE, :].T
        out_ref[:, columns] = (others_ref[:, columns] + ladder) / (virt - occ_ref[:, columns])


def finish(totals, others, occ_energy, virt_energy):
    return pl.pallas_call(
        finish_kernel,
        out_shape=jax.ShapeDtypeStruct(others.shape, F32),
        in_specs=[whole()] * (len(totals) + 3),
        out_specs=whole(),
        compiler_params=params(),
        name="finish",
    )(*totals, others, occ_energy[None, :], virt_energy[None, :])


def shift(value, axis, size, step):
    return lax.ppermute(value, axis, [(i, (i + step) % size) for i in range(size)])


def swap_y(value, bits):
    return lax.ppermute(value, ("yh", "yl"), [(i, i ^ bits) for i in range(4)])


def along_x(value, step):
    return shift(value, "x", NX, step)


def after(value, *others):
    return lax.optimization_barrier((value, *others))[0]


def body(amplitudes, amp_mask, integrals, int_mask, others, occ_energy, virt_energy):
    def join(*values):
        return jnp.concatenate(values, axis=0)

    send, own = prepare_integrals(integrals, int_mask)
    received = shift(send, "c", 2, 1)
    width = own[0].shape[1]
    starts = [join(own[i], received[:, i * width : (i + 1) * width]) for i in range(2)]
    away = prepare_amplitudes(amplitudes, after(amp_mask, *starts), 1)
    keep = prepare_amplitudes(amplitudes, after(amp_mask, away), 0)
    other_rows = swap_y(away, 2)

    chains = [[start] for start in starts]
    ends = [[start, start] for start in starts]
    for step in range(3):
        ends = [[shift(up, "z", NZ, 1), shift(down, "z", NZ, -1)] for up, down in ends]
        if step == 0:
            ends = [[after(up, away, keep), after(down, away, keep)] for up, down in ends]
        for chain, pair in zip(chains, ends):
            chain.extend(pair)
    mine = after(join(other_rows, keep), *ends[0], *ends[1])
    chains[0].append(shift(ends[0][1], "z", NZ, -1))
    chains[1].append(shift(ends[1][0], "z", NZ, 1))
    amps = mine, shift(mine, "c", 2, 1)

    c_there, c_here = [
        (along_x(low, 1), along_x(high, -1))
        for low, high in product(amps, chains[0], 0, name="product_c")
    ]
    up, down = product(amps, chains[1], 0, joined=True, name="product_b")
    near = along_x(up, 1), along_x(down, -1)
    a_there, a_here = product(amps, chains[0], 1, name="product_a")
    far = a_here[0] + swap_y(a_here[1], 1) + swap_y(a_there[1], 3) + swap_y(a_there[0], 2)
    far = along_x(far, 2)
    d_there, d_here = product(amps, chains[1], 1, name="product_d")
    totals = [
        d_here[1],
        far,
        *c_here,
        swap_y(d_there[1] + c_there[0] + c_there[1], 2),
        swap_y(d_here[0] + near[0][1] + near[1][1], 1),
        swap_y(d_there[0] + near[0][0] + near[1][0], 3),
    ]
    return finish(totals, others, occ_energy, virt_energy)


def solution(mesh):
    fine = Mesh(mesh.devices.reshape(NZ, 2, 2, NX, 2), ("z", "yh", "yl", "x", "c"))
    row, col = ("z", "yh"), ("yl", "x", "c")
    placed = (P(row, col), P(row, col), P(col + row, None), P(), P(col, row), P(row), P(col))
    return jax.shard_map(
        body, mesh=fine, in_specs=placed, out_specs=P(col, row), check_vma=False
    )
```
